512 devices in a mesh: dp: 64 (over y, x, core), mp: 8 (over z).
Axes of the slice: x: 4, y: 8, z: 8, core: 2. Of those that a mesh axis runs over, the one named last changes fastest.
Arguments:
- hidden_acts: bfloat16 [49152, 5120], P('dp', 'mp'), may hold values from -36 to 36, as said below
- out_grads: bfloat16 [49152, 2048], P('dp', 'mp'), may hold values from -0.25 to 0.25
- prev_factor: float32 [4, 2048], replicated, may hold values from -6 to 6
Outputs:
- basis: float32 [4, 5120], P(None, 'mp')
- factor: float32 [4, 2048], replicated
- residual: bfloat16 [64, 5120, 2048], P('dp', 'mp')
The draws below stay inside these ranges and needn't reach their ends.
Inputs may be any that keep to these rules, and one draw needn't show every extreme that they name: `hidden_acts`: activations of hidden units, of varying scale from unit to unit.
All inputs are finite; a program needn't handle non-finite values.
Results may differ from the reference program's by a relative error of at most 0.00105.
Values may be sent and summed in bfloat16 or wider, within the bound.
No kernel may reach another device: no remote copies, remote signals or barrier semaphores. Data moves between devices by JAX's collectives and lax.ppermute only.
A program may use at most 64 MiB of HBM per device.

```python
import math
import jax
import jax.numpy as jnp
from jax import lax

D = 2048
FF = 5120
RANK = 4
TOK_DEV = 768
TOKENS = 49152
N_DP = 64


def token_signal(key, count):
    return jnp.clip(jax.random.normal(jax.random.fold_in(key, 101), (TOKENS, count), jnp.float32), -4.0, 4.0)


def loading_strength():
    return math.sqrt(0.75) * float(TOK_DEV) ** (-0.25)


def mixed_values(signal, loadings, noise):
    total = noise
    for k in range(loadings.shape[0]):
        total = total + signal[:, k:k + 1] * loadings[k][None, :]
    return total


def draw_hidden_acts(key, part):
    signal = token_signal(key, RANK)
    key = jax.random.fold_in(key, 11)
    scale_key, value_key, load_key = jax.random.split(key, 3)
    loadings = jax.random.normal(load_key, (RANK, FF), jnp.float32) * loading_strength()
    ramp = 1.0 + 2.0 * jnp.arange(FF, dtype=jnp.float32) / FF
    scales = jnp.exp(jax.random.uniform(scale_key, (FF,), jnp.float32, math.log(0.3), math.log(3.0))) * ramp
    noise = jnp.clip(jax.random.normal(value_key, (TOKENS, FF), jnp.float32), -4.0, 4.0)
    limit = 4.0
    values = jnp.clip(mixed_values(signal, loadings, noise), -limit, limit)
    return (values * scales[None, :]).astype(jnp.bfloat16)


def draw_out_grads(key, part):
    signal = token_signal(key, RANK)
    key = jax.random.fold_in(key, 23)
    load_key, value_key = jax.random.split(key)
    loadings = jax.random.normal(load_key, (RANK, D), jnp.float32) * loading_strength()
    noise = jnp.clip(jax.random.normal(value_key, (TOKENS, D), jnp.float32), -4.0, 4.0)
    limit = 4.0
    gain = 0.0625
    values = jnp.clip(mixed_values(signal, loadings, noise), -limit, limit)
    return (values * gain).astype(jnp.bfloat16)


def normal_values(key, dims, width, bound, held_as=jnp.bfloat16):
    array = jax.random.normal(key, dims, jnp.float32) * width
    return jnp.minimum(jnp.maximum(array, -bound), bound).astype(held_as)


def setup_inputs(seed: int = 0) -> dict:
    keys = jax.random.split(jax.random.key(seed), 4)
    return {
        "hidden_acts": draw_hidden_acts(jax.random.fold_in(keys[3], 71), 0),
        "out_grads": draw_out_grads(jax.random.fold_in(keys[3], 71), 0),
        "prev_factor": normal_values(keys[2], (RANK, D), 1.0, 6.0, jnp.float32),
    }


def orthonormal(raw):
    rows = []
    for k in range(raw.shape[0]):
        vector = raw[k]
        if rows:
            stack = jnp.stack(rows)
            weights = jnp.dot(stack, vector, precision=lax.Precision.HIGHEST)
            vector = vector - jnp.dot(weights, stack, precision=lax.Precision.HIGHEST)
        rows.append(vector * lax.rsqrt(jnp.sum(vector * vector) + 1e-06))
    return jnp.stack(rows)

def reference(hidden_acts, out_grads, prev_factor):
    acts = hidden_acts.reshape(N_DP, TOK_DEV, FF)
    grads = out_grads.reshape(N_DP, TOK_DEV, D)

    def left_part(pair):
        act_block, grad_block = pair
        coeffs = jnp.dot(prev_factor, grad_block.astype(jnp.float32).T, precision=lax.Precision.HIGHEST)
        return jnp.dot(coeffs, act_block.astype(jnp.float32), precision=lax.Precision.HIGHEST)
    raw = lax.optimization_barrier(jnp.sum(lax.map(left_part, (acts, grads)), axis=0)) / N_DP
    unit_rows = orthonormal(raw)

    def right_part(pair):
        act_block, grad_block = pair
        coeffs = jnp.dot(unit_rows, act_block.astype(jnp.float32).T, precision=lax.Precision.HIGHEST)
        return jnp.dot(coeffs, grad_block.astype(jnp.float32), precision=lax.Precision.HIGHEST)
    factor = lax.optimization_barrier(jnp.sum(lax.map(right_part, (acts, grads)), axis=0)) / N_DP
    approx = jnp.dot(unit_rows.T, factor, precision=lax.Precision.HIGHEST)

    def leftover(pair):
        act_block, grad_block = pair
        whole = jnp.dot(act_block.T, grad_block, preferred_element_type=jnp.float32)
        return (whole - approx).astype(jnp.bfloat16)
    residual = lax.map(leftover, (acts, grads))
    return (unit_rows * math.sqrt(FF), factor, residual)
```

```python
import functools
import math

import jax
import jax.numpy as jnp
from jax import lax
from jax.experimental import pallas as pl
from jax.experimental.pallas import tpu as pltpu
from jax.sharding import PartitionSpec as P

F32 = jnp.float32
BF16 = jnp.bfloat16
VMEM_BYTES = 40 * 1024 * 1024
PIECE_PAIRS = ((0, 0), (0, 1), (1, 0), (0, 2), (1, 1), (2, 0))


def pieces(x):
    high = x.astype(BF16).astype(F32)
    rest = x - high
    middle = rest.astype(BF16).astype(F32)
    low = (rest - middle).astype(BF16).astype(F32)
    return high, middle, low


def tree_sum(values):
    values = list(values)
    while len(values) > 1:
        values = [values[i] + values[i + 1] for i in range(0, len(values), 2)]
    return values[0]


def fold(product, rank):
    return product[:rank] + (product[rank:2 * rank] + product[2 * rank:3 * rank])


def stack_pieces(x, stack):
    rank = x.shape[0]
    stack[...] = jnp.zeros_like(stack)
    for i, piece in enumerate(pieces(x)):
        stack[rank * i:rank * (i + 1), :] = piece
    return stack[...].astype(BF16)


def coeff_kernel(prev_ref, grads_ref, out_ref, stack):
    width = grads_ref.shape[1]
    start = pl.multiple_of(lax.axis_index("mp") * width, width)
    rows = stack_pieces(prev_ref[:, pl.ds(start, width)], stack)
    product = lax.dot_general(
        rows, grads_ref[...], (((1,), (1,)), ((), ())), preferred_element_type=F32
    )
    out_ref[...] = fold(product, prev_ref.shape[0])


def left_kernel(*refs):
    *parts, acts_ref, out_ref, stack = refs
    rows = stack_pieces(tree_sum([p[...] for p in parts]), stack)
    product = jnp.dot(rows, acts_ref[...], preferred_element_type=F32)
    out_ref[...] = fold(product, out_ref.shape[0])


def back_kernel(scale, *refs):
    *parts, acts_ref, out_ref, stack = refs
    units = acts_ref.shape[1]
    raw = tree_sum([p[...] for p in parts]) * scale
    rows = stack_pieces(raw, stack)
    product = lax.dot_general(
        rows, acts_ref[...], (((1,), (1,)), ((), ())), preferred_element_type=F32
    )
    out_ref[:, :units] = raw
    out_ref[:, units:] = fold(product, out_ref.shape[0])


def right_kernel(units, *refs):
    *parts, grads_ref, out_ref, stack = refs
    rows = stack_pieces(tree_sum([p[:, units:] for p in parts]), stack)
    product = jnp.dot(rows, grads_ref[...], preferred_element_type=F32)
    out_ref[...] = fold(product, out_ref.shape[0])


def total(x):
    return jnp.sum(jnp.sum(x, axis=1, keepdims=True), axis=0, keepdims=True)


def basis_kernel(units, full_units, *refs):
    *parts, basis_ref, wide_ref, map_ref, rows, unit = refs
    rank = basis_ref.shape[0]
    me = lax.axis_index("mp")
    for k, part in enumerate(parts):
        place = jnp.bitwise_xor(me, k)
        for r in range(rank):
            rows[r, pl.ds(place, 1), :] = part[r:r + 1, :units]
    units_done, maps = [], []
    for k in range(rank):
        raw = rows[k]
        vector = raw
        line = [jnp.full((1, 1), 1.0 if j == k else 0.0, F32) for j in range(rank)]
        if k:
            weights = [total(u * raw) for u in units_done]
            vector = raw - functools.reduce(
                jnp.add, [w * u for w, u in zip(weights, units_done)]
            )
            for w, earlier in zip(weights, maps):
                line = [a - w * b for a, b in zip(line, earlier)]
        square = total(vector * vector) + 1e-06
        inverse = lax.rsqrt(square)
        inverse = inverse * (1.5 - 0.5 * (square * inverse) * inverse)
        units_done.append(vector * inverse)
        maps.append([a * inverse for a in line])
        unit[k] = units_done[k]
        for j in range(rank):
            map_ref[rank * k + j:rank * k + j + 1, :] = jnp.broadcast_to(maps[k][j], (1, 128))
    wide_ref[...] = jnp.zeros_like(wide_ref)
    for k in range(rank):
        mine = unit[k, pl.ds(me, 1), :]
        basis_ref[k:k + 1, :] = mine * math.sqrt(full_units)
        split = pieces(mine)
        for i, (a, _) in enumerate(PIECE_PAIRS):
            wide_ref[rank * i + k:rank * i + k + 1, :] = split[a]


def residual_kernel(scale, *refs):
    *parts, acts_ref, grads_ref, wide_ref, map_ref, factor_ref, out_ref, held = refs
    rank = factor_ref.shape[0]

    @pl.when(pl.program_id(0) == 0)
    def _():
        y = tree_sum([p[...] for p in parts]) * scale
        held[...] = jnp.zeros_like(held)
        for k in range(rank):
            line = functools.reduce(
                jnp.add,
                [map_ref[rank * k + j:rank * k + j + 1, 0:1] * y[j:j + 1] for j in range(rank)],
            )
            factor_ref[k:k + 1, :] = line
            split = pieces(line)
            for i, (_, b) in enumerate(PIECE_PAIRS):
                held[rank * i + k:rank * i + k + 1, :] = split[b]

    first = (((0,), (0,)), ((), ()))
    whole = lax.dot_general(acts_ref[...], grads_ref[...], first, preferred_element_type=F32)
    approx = lax.dot_general(
        wide_ref[...].astype(BF16), held[...].astype(BF16), first, preferred_element_type=F32
    )
    out_ref[0] = (whole - approx).astype(out_ref.dtype)


def call(kernel, outs, args, scratch, flops, grid=None):
    moved = sum(a.size * a.dtype.itemsize for a in args)
    moved += sum(o.size * o.dtype.itemsize for o in outs)
    single = len(outs) == 1
    return pl.pallas_call(
        kernel,
        out_shape=outs[0] if single else outs,
        scratch_shapes=scratch,
        compiler_params=pltpu.CompilerParams(vmem_limit_bytes=VMEM_BYTES),
        cost_estimate=pl.CostEstimate(flops=flops, bytes_accessed=moved, transcendentals=0),
        **(grid or {}),
    )(*args)


def exchange(x, axis, masks):
    size = lax.axis_size(axis)
    return [
        x if mask == 0 else lax.ppermute(x, axis, [(i, i ^ mask) for i in range(size)])
        for mask in masks
    ]


def local(hidden_acts, out_grads, prev_factor):
    tokens, units = hidden_acts.shape
    rank, width = prev_factor.shape
    replicas = lax.axis_size("dp")
    ways = lax.axis_size("mp")
    rows = lambda n: pltpu.VMEM((16, n), F32)
    shape = lambda *dims: jax.ShapeDtypeStruct(dims, F32)

    grads = lax.all_gather(out_grads, "mp", axis=1, tiled=True)

    coeffs = call(
        coeff_kernel, [shape(rank, tokens)], [prev_factor, out_grads],
        [rows(out_grads.shape[1])], 32 * tokens * out_grads.shape[1],
    )
    coeffs = exchange(coeffs, "mp", range(ways))
    left = call(
        left_kernel, [shape(rank, units)], [*coeffs, hidden_acts],
        [rows(tokens)], 32 * tokens * units,
    )
    for mask in (1, 2, 6, 8, 16):
        left = tree_sum(exchange(left, "dp", (0, mask)))
    packed = call(
        functools.partial(back_kernel, 1.0 / replicas), [shape(rank, units + tokens)],
        [*exchange(left, "dp", (0, 48)), hidden_acts],
        [rows(units)], 32 * tokens * units,
    )
    packed = exchange(packed, "mp", range(ways))
    right = call(
        functools.partial(right_kernel, units), [shape(rank, width)], [*packed, grads],
        [rows(tokens)], 32 * tokens * width,
    )
    basis, wide, maps = call(
        functools.partial(basis_kernel, units, units * ways),
        [shape(rank, units), shape(32, units), shape(rank * rank, 128)], packed,
        [pltpu.VMEM((rank, ways, units), F32), pltpu.VMEM((rank, ways, units), F32)],
        100 * ways * units,
    )
    right = tree_sum(exchange(right, "dp", (0, 1)))
    right = tree_sum(exchange(right, "dp", (0, 2, 4, 6)))
    right = exchange(right, "dp", range(0, 64, 8))

    tile = 128
    whole = lambda *dims: pl.BlockSpec(dims, lambda i: (0,) * len(dims))
    factor, residual = call(
        functools.partial(residual_kernel, 1.0 / replicas),
        [shape(rank, width), jax.ShapeDtypeStruct((1, units, width), BF16)],
        [*right, hidden_acts, grads, wide, maps],
        [pltpu.VMEM((32, width), F32)],
        2 * tokens * units * width,
        dict(
            grid=(units // tile,),
            in_specs=[whole(rank, width)] * len(right) + [
                pl.BlockSpec((tokens, tile), lambda i: (0, i)),
                whole(tokens, width),
                pl.BlockSpec((32, tile), lambda i: (0, i)),
                whole(rank * rank, 128),
            ],
            out_specs=[whole(rank, width), pl.BlockSpec((1, tile, width), lambda i: (0, i, 0))],
        ),
    )
    return basis, factor, residual


def solution(mesh):
    return jax.shard_map(
        local,
        mesh=mesh,
        in_specs=(P("dp", "mp"), P("dp", "mp"), P()),
        out_specs=(P(None, "mp"), P(), P("dp", "mp", None)),
        check_vma=False,
    )
```

```python
import functools
import math

import jax
import jax.numpy as jnp
from jax import lax
from jax.experimental import pallas as pl
from jax.experimental.pallas import tpu as pltpu
from jax.sharding import Mesh
from jax.sharding import PartitionSpec as P

F32 = jnp.float32
BF16 = jnp.bfloat16
VMEM_BYTES = 24 * 1024 * 1024
PIECE_PAIRS = ((0, 0), (0, 1), (1, 0), (0, 2), (1, 1), (2, 0))


def pieces(x):
    high = x.astype(BF16).astype(F32)
    rest = x - high
    middle = rest.astype(BF16).astype(F32)
    low = (rest - middle).astype(BF16).astype(F32)
    return high, middle, low


def spread(out_ref, value):
    out_ref[...] = jnp.broadcast_to(value[None], out_ref.shape)


def fold(product, rank):
    return product[:rank] + (product[rank:2 * rank] + product[2 * rank:3 * rank])


def stack_pieces(x, stack):
    rank = x.shape[0]
    stack[...] = jnp.zeros_like(stack)
    for i, piece in enumerate(pieces(x)):
        stack[rank * i:rank * (i + 1), :] = piece
    return stack[...].astype(BF16)


def coeff_kernel(prev_ref, grads_ref, out_ref, stack):
    width = grads_ref.shape[1]
    start = pl.multiple_of(lax.axis_index("mp") * width, width)
    rows = stack_pieces(prev_ref[:, pl.ds(start, width)], stack)
    product = lax.dot_general(
        rows, grads_ref[...], (((1,), (1,)), ((), ())), preferred_element_type=F32
    )
    spread(out_ref, fold(product, prev_ref.shape[0]))


def left_kernel(parts_ref, acts_ref, out_ref, stack):
    rows = stack_pieces(jnp.sum(parts_ref[...], axis=0), stack)
    product = jnp.dot(rows, acts_ref[...], preferred_element_type=F32)
    spread(out_ref, fold(product, parts_ref.shape[1]))


def sum_kernel(parts_ref, out_ref):
    spread(out_ref, jnp.sum(parts_ref[...], axis=0))


def back_kernel(scale, parts_ref, acts_ref, out_ref, stack):
    units = acts_ref.shape[1]
    raw = jnp.sum(parts_ref[...], axis=0) * scale
    rows = stack_pieces(raw, stack)
    product = lax.dot_general(
        rows, acts_ref[...], (((1,), (1,)), ((), ())), preferred_element_type=F32
    )
    ways = out_ref.shape[0]
    out_ref[:, :, :units] = jnp.broadcast_to(raw[None], (ways, *raw.shape))
    result = fold(product, raw.shape[0])
    out_ref[:, :, units:] = jnp.broadcast_to(result[None], (ways, *result.shape))


def right_kernel(units, parts_ref, grads_ref, out_ref, stack):
    rows = stack_pieces(jnp.sum(parts_ref[:, :, units:], axis=0), stack)
    product = jnp.dot(rows, grads_ref[...], preferred_element_type=F32)
    spread(out_ref, fold(product, parts_ref.shape[1]))


def total(x):
    return jnp.sum(jnp.sum(x, axis=1, keepdims=True), axis=0, keepdims=True)


def basis_kernel(units, full_units, parts_ref, basis_ref, wide_ref, map_ref, rows, unit):
    ways, rank, _ = parts_ref.shape
    me = lax.axis_index("mp")
    for k in range(ways):
        for r in range(rank):
            rows[r, k:k + 1, :] = parts_ref[k, r:r + 1, :units]
    units_done, maps = [], []
    for k in range(rank):
        raw = rows[k]
        vector = raw
        line = [jnp.full((1, 1), 1.0 if j == k else 0.0, F32) for j in range(rank)]
        if k:
            weights = [total(u * raw) for u in units_done]
            vector = raw - functools.reduce(
                jnp.add, [w * u for w, u in zip(weights, units_done)]
            )
            for w, earlier in zip(weights, maps):
                line = [a - w * b for a, b in zip(line, earlier)]
        square = total(vector * vector) + 1e-06
        inverse = lax.rsqrt(square)
        inverse = inverse * (1.5 - 0.5 * (square * inverse) * inverse)
        units_done.append(vector * inverse)
        maps.append([a * inverse for a in line])
        unit[k] = units_done[k]
        for j in range(rank):
            map_ref[rank * k + j:rank * k + j + 1, :] = jnp.broadcast_to(maps[k][j], (1, 128))
    wide_ref[...] = jnp.zeros_like(wide_ref)
    for k in range(rank):
        mine = unit[k, pl.ds(me, 1), :]
        basis_ref[k:k + 1, :] = mine * math.sqrt(full_units)
        split = pieces(mine)
        for i, (a, _) in enumerate(PIECE_PAIRS):
            wide_ref[rank * i + k:rank * i + k + 1, :] = split[a]


def residual_kernel(
    scale, parts_ref, acts_ref, grads_ref, wide_ref, map_ref, factor_ref, out_ref, held
):
    ways, rank, _ = parts_ref.shape

    @pl.when(pl.program_id(0) == 0)
    def _():
        y = jnp.concatenate([parts_ref[i] for i in range(ways)], axis=1) * scale
        held[...] = jnp.zeros_like(held)
        for k in range(rank):
            line = functools.reduce(
                jnp.add,
                [map_ref[rank * k + j:rank * k + j + 1, 0:1] * y[j:j + 1] for j in range(rank)],
            )
            factor_ref[k:k + 1, :] = line
            split = pieces(line)
            for i, (_, b) in enumerate(PIECE_PAIRS):
                held[rank * i + k:rank * i + k + 1, :] = split[b]

    first = (((0,), (0,)), ((), ()))
    whole = lax.dot_general(acts_ref[...], grads_ref[...], first, preferred_element_type=F32)
    approx = lax.dot_general(
        wide_ref[...].astype(BF16), held[...].astype(BF16), first, preferred_element_type=F32
    )
    out_ref[0] = (whole - approx).astype(out_ref.dtype)


def call(kernel, outs, args, scratch, flops, grid=None):
    moved = sum(a.size * a.dtype.itemsize for a in args)
    moved += sum(o.size * o.dtype.itemsize for o in outs)
    single = len(outs) == 1
    return pl.pallas_call(
        kernel,
        out_shape=outs[0] if single else outs,
        scratch_shapes=scratch,
        compiler_params=pltpu.CompilerParams(vmem_limit_bytes=VMEM_BYTES),
        cost_estimate=pl.CostEstimate(flops=flops, bytes_accessed=moved, transcendentals=0),
        **(grid or {}),
    )(*args)


def exchange(copies, axis):
    return lax.all_to_all(copies, axis, 0, 0, tiled=True)


def local(hidden_acts, out_grads, prev_factor):
    tokens, units = hidden_acts.shape
    rank, width = prev_factor.shape
    ways, near, far = (lax.axis_size(a) for a in ("mp", "near", "far"))
    replicas = near * far
    part = width // ways
    rows = lambda n: pltpu.VMEM((16, n), F32)
    shape = lambda *dims: jax.ShapeDtypeStruct(dims, F32)

    grads = lax.all_gather(out_grads, "mp", axis=1, tiled=True)

    coeffs = call(
        coeff_kernel, [shape(ways, rank, tokens)], [prev_factor, out_grads],
        [rows(part)], 32 * tokens * part,
    )
    left = call(
        left_kernel, [shape(near, rank, units)], [exchange(coeffs, "mp"), hidden_acts],
        [rows(tokens)], 32 * tokens * units,
    )
    left = call(sum_kernel, [shape(far, rank, units)], [exchange(left, "near")], [], 8 * units)
    packed = call(
        functools.partial(back_kernel, 1.0 / replicas), [shape(ways, rank, units + tokens)],
        [exchange(left, "far"), hidden_acts], [rows(units)], 32 * tokens * units,
    )
    packed = exchange(packed, "mp")
    right = call(
        functools.partial(right_kernel, units), [shape(near, rank, part)],
        [packed, out_grads], [rows(tokens)], 32 * tokens * part,
    )
    basis, wide, maps = call(
        functools.partial(basis_kernel, units, units * ways),
        [shape(rank, units), shape(32, units), shape(rank * rank, 128)], [packed],
        [pltpu.VMEM((rank, ways, units), F32), pltpu.VMEM((rank, ways, units), F32)],
        100 * ways * units,
    )
    right = call(sum_kernel, [shape(far, rank, part)], [exchange(right, "near")], [], 8 * part)
    right = call(sum_kernel, [shape(ways, rank, part)], [exchange(right, "far")], [], 8 * part)
    right = exchange(right, "mp")

    tile = 128
    whole = lambda *dims: pl.BlockSpec(dims, lambda i: (0,) * len(dims))
    factor, residual = call(
        functools.partial(residual_kernel, 1.0 / replicas),
        [shape(rank, width), jax.ShapeDtypeStruct((1, units, width), BF16)],
        [right, hidden_acts, grads, wide, maps],
        [pltpu.VMEM((32, width), F32)],
        2 * tokens * units * width,
        dict(
            grid=(units // tile,),
            in_specs=[
                whole(ways, rank, part),
                pl.BlockSpec((tokens, tile), lambda i: (0, i)),
                whole(tokens, width),
                pl.BlockSpec((32, tile), lambda i: (0, i)),
                whole(rank * rank, 128),
            ],
            out_specs=[whole(rank, width), pl.BlockSpec((1, tile, width), lambda i: (0, i, 0))],
        ),
    )
    return basis, factor, residual


def solution(mesh):
    replicas, ways = mesh.devices.shape
    far = 8 if replicas % 8 == 0 else 1
    split = Mesh(mesh.devices.reshape(far, replicas // far, ways), ("far", "near", "mp"))
    dp = ("far", "near")
    return jax.shard_map(
        local,
        mesh=split,
        in_specs=(P(dp, "mp"), P(dp, "mp"), P()),
        out_specs=(P(None, "mp"), P(), P(dp, "mp", None)),
        check_vma=False,
    )
```

```python
import functools
import math

import jax
import jax.numpy as jnp
from jax import lax
from jax.experimental import pallas as pl
from jax.experimental.pallas import tpu as pltpu
from jax.sharding import Mesh
from jax.sharding import PartitionSpec as P

F32 = jnp.float32
BF16 = jnp.bfloat16
VMEM_BYTES = 24 * 1024 * 1024
PIECE_PAIRS = ((0, 0), (0, 1), (1, 0), (0, 2), (1, 1), (2, 0))


def pieces(x):
    high = x.astype(BF16).astype(F32)
    rest = x - high
    middle = rest.astype(BF16).astype(F32)
    low = (rest - middle).astype(BF16).astype(F32)
    return high, middle, low


def spread(out_ref, value):
    out_ref[...] = jnp.broadcast_to(value[None], out_ref.shape)


def fold(product, rank):
    return product[:rank] + (product[rank:2 * rank] + product[2 * rank:3 * rank])


def stack_pieces(x, stack):
    rank = x.shape[0]
    stack[...] = jnp.zeros_like(stack)
    for i, piece in enumerate(pieces(x)):
        stack[rank * i:rank * (i + 1), :] = piece
    return stack[...].astype(BF16)


def coeff_kernel(prev_ref, grads_ref, out_ref, stack):
    width = grads_ref.shape[1]
    start = pl.multiple_of(lax.axis_index("mp") * width, width)
    rows = stack_pieces(prev_ref[:, pl.ds(start, width)], stack)
    product = lax.dot_general(
        rows, grads_ref[...], (((1,), (1,)), ((), ())), preferred_element_type=F32
    )
    spread(out_ref, fold(product, prev_ref.shape[0]))


def left_kernel(parts_ref, acts_ref, out_ref, stack):
    rows = stack_pieces(jnp.sum(parts_ref[...], axis=0), stack)
    product = jnp.dot(rows, acts_ref[...], preferred_element_type=F32)
    spread(out_ref, fold(product, parts_ref.shape[1]))


def sum_kernel(parts_ref, out_ref):
    spread(out_ref, jnp.sum(parts_ref[...], axis=0))


def back_kernel(scale, parts_ref, acts_ref, out_ref, stack):
    units = acts_ref.shape[1]
    raw = jnp.sum(parts_ref[...], axis=0) * scale
    rows = stack_pieces(raw, stack)
    product = lax.dot_general(
        rows, acts_ref[...], (((1,), (1,)), ((), ())), preferred_element_type=F32
    )
    ways = out_ref.shape[0]
    out_ref[:, :, :units] = jnp.broadcast_to(raw[None], (ways, *raw.shape))
    result = fold(product, raw.shape[0])
    out_ref[:, :, units:] = jnp.broadcast_to(result[None], (ways, *result.shape))


def right_kernel(units, parts_ref, grads_ref, out_ref, stack):
    rows = stack_pieces(jnp.sum(parts_ref[:, :, units:], axis=0), stack)
    product = jnp.dot(rows, grads_ref[...], preferred_element_type=F32)
    spread(out_ref, fold(product, parts_ref.shape[1]))


def total(x):
    return jnp.sum(jnp.sum(x, axis=1, keepdims=True), axis=0, keepdims=True)


def basis_kernel(units, full_units, parts_ref, basis_ref, wide_ref, map_ref, rows, unit):
    ways, rank, _ = parts_ref.shape
    me = lax.axis_index("mp")
    for k in range(ways):
        for r in range(rank):
            rows[r, k:k + 1, :] = parts_ref[k, r:r + 1, :units]
    units_done, maps = [], []
    for k in range(rank):
        raw = rows[k]
        vector = raw
        line = [jnp.full((1, 1), 1.0 if j == k else 0.0, F32) for j in range(rank)]
        if k:
            weights = [total(u * raw) for u in units_done]
            vector = raw - functools.reduce(
                jnp.add, [w * u for w, u in zip(weights, units_done)]
            )
            for w, earlier in zip(weights, maps):
                line = [a - w * b for a, b in zip(line, earlier)]
        square = total(vector * vector) + 1e-06
        inverse = lax.rsqrt(square)
        inverse = inverse * (1.5 - 0.5 * (square * inverse) * inverse)
        units_done.append(vector * inverse)
        maps.append([a * inverse for a in line])
        unit[k] = units_done[k]
        for j in range(rank):
            map_ref[rank * k + j:rank * k + j + 1, :] = jnp.broadcast_to(maps[k][j], (1, 128))
    wide_ref[...] = jnp.zeros_like(wide_ref)
    for k in range(rank):
        mine = unit[k, pl.ds(me, 1), :]
        basis_ref[k:k + 1, :] = mine * math.sqrt(full_units)
        split = pieces(mine)
        for i, (a, _) in enumerate(PIECE_PAIRS):
            wide_ref[rank * i + k:rank * i + k + 1, :] = split[a]


def gradient_kernel(acts_ref, grads_ref, out_ref):
    width = grads_ref.shape[2]
    for i in range(grads_ref.shape[0]):
        out_ref[:, i * width:(i + 1) * width] = lax.dot_general(
            acts_ref[...], grads_ref[i], (((0,), (0,)), ((), ())), preferred_element_type=F32
        )


def residual_kernel(
    scale, tile, parts_ref, whole_ref, wide_ref, map_ref, factor_ref, out_ref, held, rounded, sems
):
    ways, rank, _ = parts_ref.shape
    y = jnp.concatenate([parts_ref[i] for i in range(ways)], axis=1) * scale
    held[...] = jnp.zeros_like(held)
    for k in range(rank):
        line = functools.reduce(
            jnp.add,
            [map_ref[rank * k + j:rank * k + j + 1, 0:1] * y[j:j + 1] for j in range(rank)],
        )
        factor_ref[k:k + 1, :] = line
        split = pieces(line)
        for i, (_, b) in enumerate(PIECE_PAIRS):
            held[rank * i + k:rank * i + k + 1, :] = split[b]
    rows = held[...].astype(BF16)
    copies = []
    for i in range(whole_ref.shape[0] // tile):
        span = slice(i * tile, (i + 1) * tile)
        approx = lax.dot_general(
            wide_ref[:, span].astype(BF16), rows, (((0,), (0,)), ((), ())),
            preferred_element_type=F32,
        )
        rounded[span] = (whole_ref[span] - approx).astype(rounded.dtype)
        place = pl.ds(i * tile, tile)
        copies.append(pltpu.make_async_copy(rounded.at[place], out_ref.at[0, place], sems.at[i]))
        copies[-1].start()
    for copy in copies:
        copy.wait()


def call(kernel, outs, args, scratch, flops, grid=None):
    moved = sum(a.size * a.dtype.itemsize for a in args)
    moved += sum(o.size * o.dtype.itemsize for o in outs)
    single = len(outs) == 1
    return pl.pallas_call(
        kernel,
        out_shape=outs[0] if single else outs,
        scratch_shapes=scratch,
        compiler_params=pltpu.CompilerParams(vmem_limit_bytes=VMEM_BYTES),
        cost_estimate=pl.CostEstimate(flops=flops, bytes_accessed=moved, transcendentals=0),
        **(grid or {}),
    )(*args)


def exchange(copies, axis):
    return lax.all_to_all(copies, axis, 0, 0, tiled=True)


def local(hidden_acts, out_grads, prev_factor):
    tokens, units = hidden_acts.shape
    rank, width = prev_factor.shape
    ways, near, far = (lax.axis_size(a) for a in ("mp", "near", "far"))
    replicas = near * far
    part = width // ways
    rows = lambda n: pltpu.VMEM((16, n), F32)
    shape = lambda *dims: jax.ShapeDtypeStruct(dims, F32)

    grads = lax.all_gather(out_grads, "mp", axis=0)
    hbm = pl.BlockSpec(memory_space=pltpu.HBM)
    vmem = pl.BlockSpec(memory_space=pltpu.VMEM)
    sems = pltpu.SemaphoreType.DMA

    coeffs = call(
        coeff_kernel, [shape(ways, rank, tokens)], [prev_factor, out_grads],
        [rows(part)], 32 * tokens * part,
    )
    left = call(
        left_kernel, [shape(near, rank, units)], [exchange(coeffs, "mp"), hidden_acts],
        [rows(tokens)], 32 * tokens * units,
    )
    left = call(sum_kernel, [shape(far, rank, units)], [exchange(left, "near")], [], 8 * units)
    packed = call(
        functools.partial(back_kernel, 1.0 / replicas), [shape(ways, rank, units + tokens)],
        [exchange(left, "far"), hidden_acts], [rows(units)], 32 * tokens * units,
    )
    packed = exchange(packed, "mp")
    right = call(
        functools.partial(right_kernel, units), [shape(near, rank, part)],
        [packed, out_grads], [rows(tokens)], 32 * tokens * part,
    )
    basis, wide, maps = call(
        functools.partial(basis_kernel, units, units * ways),
        [shape(rank, units), shape(32, units), shape(rank * rank, 128)], [packed],
        [pltpu.VMEM((rank, ways, units), F32), pltpu.VMEM((rank, ways, units), F32)],
        100 * ways * units,
    )
    right = call(sum_kernel, [shape(far, rank, part)], [exchange(right, "near")], [], 8 * part)
    right = call(sum_kernel, [shape(ways, rank, part)], [exchange(right, "far")], [], 8 * part)
    right = exchange(right, "mp")

    tile = 128
    gradient = call(
        gradient_kernel, [shape(units, width)], [hidden_acts, grads], [],
        2 * tokens * units * width,
        dict(
            grid=(units // tile,),
            in_specs=[
                pl.BlockSpec((tokens, tile), lambda i: (0, i)),
                pl.BlockSpec((ways, tokens, part), lambda i: (0, 0, 0)),
            ],
            out_specs=pl.BlockSpec((tile, width), lambda i: (i, 0)),
        ),
    )
    factor, residual = call(
        functools.partial(residual_kernel, 1.0 / replicas, tile),
        [shape(rank, width), jax.ShapeDtypeStruct((1, units, width), BF16)],
        [right, gradient, wide, maps],
        [pltpu.VMEM((32, width), F32), pltpu.VMEM((units, width), BF16), sems((units // tile,))],
        64 * units * width,
        dict(in_specs=[vmem] * 4, out_specs=[vmem, hbm]),
    )
    return basis, factor, residual


def solution(mesh):
    replicas, ways = mesh.devices.shape
    far = 8 if replicas % 8 == 0 else 1
    split = Mesh(mesh.devices.reshape(far, replicas // far, ways), ("far", "near", "mp"))
    dp = ("far", "near")
    return jax.shard_map(
        local,
        mesh=split,
        in_specs=(P(dp, "mp"), P(dp, "mp"), P()),
        out_specs=(P(None, "mp"), P(), P(dp, "mp", None)),
        check_vma=False,
    )
```

```python
import functools
import math

import jax
import jax.numpy as jnp
from jax import lax
from jax.experimental import pallas as pl
from jax.experimental.pallas import tpu as pltpu
from jax.sharding import Mesh
from jax.sharding import PartitionSpec as P

F32 = jnp.float32
BF16 = jnp.bfloat16
VMEM_BYTES = 24 * 1024 * 1024
PIECE_PAIRS = ((0, 0), (0, 1), (1, 0), (0, 2), (1, 1), (2, 0))


def pieces(x):
    high = x.astype(BF16).astype(F32)
    rest = x - high
    middle = rest.astype(BF16).astype(F32)
    low = (rest - middle).astype(BF16).astype(F32)
    return high, middle, low


def spread(out_ref, value):
    out_ref[...] = jnp.broadcast_to(value[None], out_ref.shape)


def fold(product, rank):
    return product[:rank] + (product[rank:2 * rank] + product[2 * rank:3 * rank])


def stack_pieces(x, stack):
    rank = x.shape[0]
    stack[...] = jnp.zeros_like(stack)
    for i, piece in enumerate(pieces(x)):
        stack[rank * i:rank * (i + 1), :] = piece
    return stack[...].astype(BF16)


def coeff_kernel(prev_ref, grads_ref, out_ref, stack):
    width = grads_ref.shape[1]
    start = pl.multiple_of(lax.axis_index("mp") * width, width)
    rows = stack_pieces(prev_ref[:, pl.ds(start, width)], stack)
    product = lax.dot_general(
        rows, grads_ref[...], (((1,), (1,)), ((), ())), preferred_element_type=F32
    )
    spread(out_ref, fold(product, prev_ref.shape[0]))


def left_kernel(parts_ref, acts_ref, out_ref, stack):
    rows = stack_pieces(jnp.sum(parts_ref[...], axis=0), stack)
    product = jnp.dot(rows, acts_ref[...], preferred_element_type=F32)
    spread(out_ref, fold(product, parts_ref.shape[1]))


def sum_kernel(parts_ref, out_ref):
    spread(out_ref, jnp.sum(parts_ref[...], axis=0))


def back_kernel(scale, parts_ref, acts_ref, out_ref, stack):
    units = acts_ref.shape[1]
    raw = jnp.sum(parts_ref[...], axis=0) * scale
    rows = stack_pieces(raw, stack)
    product = lax.dot_general(
        rows, acts_ref[...], (((1,), (1,)), ((), ())), preferred_element_type=F32
    )
    ways = out_ref.shape[0]
    out_ref[:, :, :units] = jnp.broadcast_to(raw[None], (ways, *raw.shape))
    result = fold(product, raw.shape[0])
    out_ref[:, :, units:] = jnp.broadcast_to(result[None], (ways, *result.shape))


def right_kernel(units, parts_ref, grads_ref, out_ref, stack):
    rows = stack_pieces(jnp.sum(parts_ref[:, :, units:], axis=0), stack)
    product = jnp.dot(rows, grads_ref[...], preferred_element_type=F32)
    spread(out_ref, fold(product, parts_ref.shape[1]))


def total(x):
    return jnp.sum(jnp.sum(x, axis=1, keepdims=True), axis=0, keepdims=True)


def basis_kernel(units, full_units, parts_ref, basis_ref, wide_ref, map_ref, rows, unit):
    ways, rank, _ = parts_ref.shape
    me = lax.axis_index("mp")
    for k in range(ways):
        for r in range(rank):
            rows[r, k:k + 1, :] = parts_ref[k, r:r + 1, :units]
    units_done, maps = [], []
    for k in range(rank):
        raw = rows[k]
        vector = raw
        line = [jnp.full((1, 1), 1.0 if j == k else 0.0, F32) for j in range(rank)]
        if k:
            weights = [total(u * raw) for u in units_done]
            vector = raw - functools.reduce(
                jnp.add, [w * u for w, u in zip(weights, units_done)]
            )
            for w, earlier in zip(weights, maps):
                line = [a - w * b for a, b in zip(line, earlier)]
        square = total(vector * vector) + 1e-06
        inverse = lax.rsqrt(square)
        inverse = inverse * (1.5 - 0.5 * (square * inverse) * inverse)
        units_done.append(vector * inverse)
        maps.append([a * inverse for a in line])
        unit[k] = units_done[k]
        for j in range(rank):
            map_ref[rank * k + j:rank * k + j + 1, :] = jnp.broadcast_to(maps[k][j], (1, 128))
    wide_ref[...] = jnp.zeros_like(wide_ref)
    for k in range(rank):
        mine = unit[k, pl.ds(me, 1), :]
        basis_ref[k:k + 1, :] = mine * math.sqrt(full_units)
        split = pieces(mine)
        for i, (a, _) in enumerate(PIECE_PAIRS):
            wide_ref[rank * i + k:rank * i + k + 1, :] = split[a]


def residual_kernel(
    scale, parts_ref, acts_ref, grads_ref, wide_ref, map_ref, factor_ref, out_ref,
    turned, held, rounded, sems,
):
    ways, rank, width = parts_ref.shape
    turned[...] = acts_ref[...].T
    left = wide_ref[...].astype(BF16)
    maps = [map_ref[i:i + 1, 0:1] for i in range(rank * rank)]
    copies = []
    for i in range(ways):
        span = slice(i * width, (i + 1) * width)
        y = parts_ref[i] * scale
        held[...] = jnp.zeros_like(held)
        for k in range(rank):
            line = functools.reduce(
                jnp.add, [maps[rank * k + j] * y[j:j + 1] for j in range(rank)]
            )
            factor_ref[k:k + 1, span] = line
            split = pieces(line)
            for n, (_, b) in enumerate(PIECE_PAIRS):
                held[rank * n + k:rank * n + k + 1, :] = -split[b]
        whole = jnp.dot(turned[...], grads_ref[i], preferred_element_type=F32)
        less = lax.dot_general(
            left, held[...].astype(BF16), (((0,), (0,)), ((), ())), preferred_element_type=F32
        )
        rounded[:, span] = (whole + less).astype(rounded.dtype)
        place = pl.ds(i * width, width)
        copies.append(
            pltpu.make_async_copy(rounded.at[:, place], out_ref.at[0, :, place], sems.at[i])
        )
        copies[-1].start()
    for copy in copies:
        copy.wait()


def call(kernel, outs, args, scratch, flops, grid=None):
    moved = sum(a.size * a.dtype.itemsize for a in args)
    moved += sum(o.size * o.dtype.itemsize for o in outs)
    single = len(outs) == 1
    return pl.pallas_call(
        kernel,
        out_shape=outs[0] if single else outs,
        scratch_shapes=scratch,
        compiler_params=pltpu.CompilerParams(vmem_limit_bytes=VMEM_BYTES),
        cost_estimate=pl.CostEstimate(flops=flops, bytes_accessed=moved, transcendentals=0),
        **(grid or {}),
    )(*args)


def exchange(copies, axis):
    return lax.all_to_all(copies, axis, 0, 0, tiled=True)


def local(hidden_acts, out_grads, prev_factor):
    tokens, units = hidden_acts.shape
    rank, width = prev_factor.shape
    ways, near, far = (lax.axis_size(a) for a in ("mp", "near", "far"))
    replicas = near * far
    part = width // ways
    rows = lambda n: pltpu.VMEM((16, n), F32)
    shape = lambda *dims: jax.ShapeDtypeStruct(dims, F32)

    grads = lax.all_gather(out_grads, "mp", axis=0)
    hbm = pl.BlockSpec(memory_space=pltpu.HBM)
    vmem = pl.BlockSpec(memory_space=pltpu.VMEM)
    sems = pltpu.SemaphoreType.DMA

    coeffs = call(
        coeff_kernel, [shape(ways, rank, tokens)], [prev_factor, out_grads],
        [rows(part)], 32 * tokens * part,
    )
    left = call(
        left_kernel, [shape(near, rank, units)], [exchange(coeffs, "mp"), hidden_acts],
        [rows(tokens)], 32 * tokens * units,
    )
    left = call(sum_kernel, [shape(far, rank, units)], [exchange(left, "near")], [], 8 * units)
    packed = call(
        functools.partial(back_kernel, 1.0 / replicas), [shape(ways, rank, units + tokens)],
        [exchange(left, "far"), hidden_acts], [rows(units)], 32 * tokens * units,
    )
    packed = exchange(packed, "mp")
    right = call(
        functools.partial(right_kernel, units), [shape(near, rank, part)],
        [packed, out_grads], [rows(tokens)], 32 * tokens * part,
    )
    basis, wide, maps = call(
        functools.partial(basis_kernel, units, units * ways),
        [shape(rank, units), shape(32, units), shape(rank * rank, 128)], [packed],
        [pltpu.VMEM((rank, ways, units), F32), pltpu.VMEM((rank, ways, units), F32)],
        100 * ways * units,
    )
    right = call(sum_kernel, [shape(far, rank, part)], [exchange(right, "near")], [], 8 * part)
    right = call(sum_kernel, [shape(ways, rank, part)], [exchange(right, "far")], [], 8 * part)
    right = exchange(right, "mp")

    factor, residual = call(
        functools.partial(residual_kernel, 1.0 / replicas),
        [shape(rank, width), jax.ShapeDtypeStruct((1, units, width), BF16)],
        [right, hidden_acts, grads, wide, maps],
        [
            pltpu.VMEM((units, tokens), BF16), pltpu.VMEM((32, part), F32),
            pltpu.VMEM((units, width), BF16), sems((ways,)),
        ],
        2 * tokens * units * width,
        dict(in_specs=[vmem] * 5, out_specs=[vmem, hbm]),
    )
    return basis, factor, residual


def solution(mesh):
    replicas, ways = mesh.devices.shape
    far = 8 if replicas % 8 == 0 else 1
    split = Mesh(mesh.devices.reshape(far, replicas // far, ways), ("far", "near", "mp"))
    dp = ("far", "near")
    return jax.shard_map(
        local,
        mesh=split,
        in_specs=(P(dp, "mp"), P(dp, "mp"), P()),
        out_specs=(P(None, "mp"), P(), P(dp, "mp", None)),
        check_vma=False,
    )
```

```python
import functools
import math

import jax
import jax.numpy as jnp
from jax import lax
from jax.experimental import pallas as pl
from jax.experimental.pallas import tpu as pltpu
from jax.sharding import Mesh
from jax.sharding import PartitionSpec as P

F32 = jnp.float32
BF16 = jnp.bfloat16
VMEM_BYTES = 24 * 1024 * 1024
PIECE_PAIRS = ((0, 0), (0, 1), (1, 0), (0, 2), (1, 1), (2, 0))


def pieces(x):
    high = x.astype(BF16).astype(F32)
    rest = x - high
    middle = rest.astype(BF16).astype(F32)
    low = (rest - middle).astype(BF16).astype(F32)
    return high, middle, low


def spread(out_ref, value):
    out_ref[...] = jnp.broadcast_to(value[None], out_ref.shape)


def fold(product, rank):
    return product[:rank] + (product[rank:2 * rank] + product[2 * rank:3 * rank])


def stack_pieces(x, stack):
    rank = x.shape[0]
    stack[...] = jnp.zeros_like(stack)
    for i, piece in enumerate(pieces(x)):
        stack[rank * i:rank * (i + 1), :] = piece
    return stack[...].astype(BF16)


def coeff_kernel(prev_ref, grads_ref, out_ref, stack):
    width = grads_ref.shape[1]
    start = pl.multiple_of(lax.axis_index("mp") * width, width)
    rows = stack_pieces(prev_ref[:, pl.ds(start, width)], stack)
    product = lax.dot_general(
        rows, grads_ref[...], (((1,), (1,)), ((), ())), preferred_element_type=F32
    )
    spread(out_ref, fold(product, prev_ref.shape[0]))


def left_kernel(parts_ref, acts_ref, out_ref, stack):
    rows = stack_pieces(jnp.sum(parts_ref[...], axis=0), stack)
    product = jnp.dot(rows, acts_ref[...], preferred_element_type=F32)
    spread(out_ref, fold(product, parts_ref.shape[1]))


def sum_kernel(parts_ref, out_ref):
    spread(out_ref, jnp.sum(parts_ref[...], axis=0))


def total(x):
    return jnp.sum(jnp.sum(x, axis=1, keepdims=True), axis=0, keepdims=True)


def inverse_root(square):
    inverse = lax.rsqrt(square)
    return inverse * (1.5 - 0.5 * (square * inverse) * inverse)


def triangle(raw):
    rank = raw.shape[0]
    rows = [raw[k:k + 1] for k in range(rank)]
    lane = lax.broadcasted_iota(jnp.int32, (1, 128), 1)
    lines = [jnp.zeros((1, 128), F32) for _ in range(rank)]
    for j in range(rank):
        square = total(rows[j] * rows[j])
        inverse = jnp.where(square > 0.0, inverse_root(square), 0.0)
        unit = rows[j] * inverse
        lines[j] = jnp.where(lane == j, square * inverse, lines[j])
        for k in range(j + 1, rank):
            weight = total(rows[k] * unit)
            rows[k] = rows[k] - weight * unit
            lines[k] = jnp.where(lane == j, weight, lines[k])
    return lines


def back_kernel(scale, parts_ref, acts_ref, raw_ref, out_ref, stack):
    tokens = acts_ref.shape[0]
    raw = jnp.sum(parts_ref[...], axis=0) * scale
    raw_ref[...] = raw
    rows = stack_pieces(raw, stack)
    product = lax.dot_general(
        rows, acts_ref[...], (((1,), (1,)), ((), ())), preferred_element_type=F32
    )
    ways, rank, _ = out_ref.shape
    result = fold(product, rank)
    out_ref[:, :, :tokens] = jnp.broadcast_to(result[None], (ways, rank, tokens))
    for k, line in enumerate(triangle(raw)):
        out_ref[:, k:k + 1, tokens:] = jnp.broadcast_to(line[None], (ways, 1, 128))


def right_kernel(parts_ref, grads_ref, out_ref, stack):
    tokens = grads_ref.shape[0]
    rows = stack_pieces(jnp.sum(parts_ref[:, :, :tokens], axis=0), stack)
    product = jnp.dot(rows, grads_ref[...], preferred_element_type=F32)
    spread(out_ref, fold(product, parts_ref.shape[1]))


def basis_kernel(
    full_units, parts_ref, raw_ref, acts_ref, basis_ref, wide_ref, map_ref, turned_ref, rows
):
    ways, rank, _ = parts_ref.shape
    tokens = acts_ref.shape[0]
    for k in range(ways):
        for r in range(rank):
            rows[r, k:k + 1, :] = parts_ref[k, r:r + 1, tokens:]
    done, mine, maps = [], [], []
    wide_ref[...] = jnp.zeros_like(wide_ref)
    for k in range(rank):
        raw = rows[k]
        vector = raw
        own = raw_ref[k:k + 1]
        line = [jnp.full((1, 1), 1.0 if j == k else 0.0, F32) for j in range(rank)]
        if k:
            weights = [total(u * raw) for u in done]
            vector = raw - functools.reduce(jnp.add, [w * u for w, u in zip(weights, done)])
            own = own - functools.reduce(jnp.add, [w * u for w, u in zip(weights, mine)])
            for w, earlier in zip(weights, maps):
                line = [a - w * b for a, b in zip(line, earlier)]
        inverse = inverse_root(total(vector * vector) + 1e-06)
        done.append(vector * inverse)
        mine.append(own * inverse)
        maps.append([a * inverse for a in line])
        for j in range(rank):
            map_ref[rank * k + j:rank * k + j + 1, :] = jnp.broadcast_to(maps[k][j], (1, 128))
        basis_ref[k:k + 1, :] = mine[k] * math.sqrt(full_units)
        split = pieces(mine[k])
        for i, (a, _) in enumerate(PIECE_PAIRS):
            wide_ref[rank * i + k:rank * i + k + 1, :] = split[a]
    turned_ref[...] = acts_ref[...].T


def residual_kernel(
    scale, parts_ref, turned_ref, grads_ref, wide_ref, map_ref, factor_ref, out_ref,
    held, rounded, sems,
):
    ways, rank, width = parts_ref.shape
    left = wide_ref[...].astype(BF16)
    maps = [map_ref[i:i + 1, 0:1] for i in range(rank * rank)]
    copies = []
    for i in range(ways):
        span = slice(i * width, (i + 1) * width)
        y = parts_ref[i] * scale
        held[...] = jnp.zeros_like(held)
        for k in range(rank):
            line = functools.reduce(
                jnp.add, [maps[rank * k + j] * y[j:j + 1] for j in range(rank)]
            )
            factor_ref[k:k + 1, span] = line
            split = pieces(line)
            for n, (_, b) in enumerate(PIECE_PAIRS):
                held[rank * n + k:rank * n + k + 1, :] = -split[b]
        whole = jnp.dot(turned_ref[...], grads_ref[i], preferred_element_type=F32)
        less = lax.dot_general(
            left, held[...].astype(BF16), (((0,), (0,)), ((), ())), preferred_element_type=F32
        )
        rounded[:, span] = (whole + less).astype(rounded.dtype)
        place = pl.ds(i * width, width)
        copies.append(
            pltpu.make_async_copy(rounded.at[:, place], out_ref.at[0, :, place], sems.at[i])
        )
        copies[-1].start()
    for copy in copies:
        copy.wait()


def call(kernel, outs, args, scratch, flops, grid=None):
    moved = sum(a.size * a.dtype.itemsize for a in args)
    moved += sum(o.size * o.dtype.itemsize for o in outs)
    single = len(outs) == 1
    return pl.pallas_call(
        kernel,
        out_shape=outs[0] if single else outs,
        scratch_shapes=scratch,
        compiler_params=pltpu.CompilerParams(vmem_limit_bytes=VMEM_BYTES),
        cost_estimate=pl.CostEstimate(flops=flops, bytes_accessed=moved, transcendentals=0),
        **(grid or {}),
    )(*args)


def exchange(copies, axis):
    return lax.all_to_all(copies, axis, 0, 0, tiled=True)


def local(hidden_acts, out_grads, prev_factor):
    tokens, units = hidden_acts.shape
    rank, width = prev_factor.shape
    ways, near, far = (lax.axis_size(a) for a in ("mp", "near", "far"))
    replicas = near * far
    part = width // ways
    rows = lambda n: pltpu.VMEM((16, n), F32)
    shape = lambda *dims: jax.ShapeDtypeStruct(dims, F32)

    grads = lax.all_gather(out_grads, "mp", axis=0)
    hbm = pl.BlockSpec(memory_space=pltpu.HBM)
    vmem = pl.BlockSpec(memory_space=pltpu.VMEM)
    sems = pltpu.SemaphoreType.DMA

    coeffs = call(
        coeff_kernel, [shape(ways, rank, tokens)], [prev_factor, out_grads],
        [rows(part)], 32 * tokens * part,
    )
    left = call(
        left_kernel, [shape(near, rank, units)], [exchange(coeffs, "mp"), hidden_acts],
        [rows(tokens)], 32 * tokens * units,
    )
    left = call(sum_kernel, [shape(far, rank, units)], [exchange(left, "near")], [], 8 * units)
    raw, packed = call(
        functools.partial(back_kernel, 1.0 / replicas),
        [shape(rank, units), shape(ways, rank, tokens + 128)],
        [exchange(left, "far"), hidden_acts], [rows(units)], 32 * tokens * units,
    )
    packed = exchange(packed, "mp")
    right = call(
        right_kernel, [shape(near, rank, part)], [packed, out_grads],
        [rows(tokens)], 32 * tokens * part,
    )
    basis, wide, maps, turned = call(
        functools.partial(basis_kernel, units * ways),
        [
            shape(rank, units), shape(32, units), shape(rank * rank, 128),
            jax.ShapeDtypeStruct((units, tokens), BF16),
        ],
        [packed, raw, hidden_acts], [pltpu.VMEM((rank, ways, 128), F32)], 100 * ways * units,
    )
    right = call(sum_kernel, [shape(far, rank, part)], [exchange(right, "near")], [], 8 * part)
    right = call(sum_kernel, [shape(ways, rank, part)], [exchange(right, "far")], [], 8 * part)
    right = exchange(right, "mp")

    factor, residual = call(
        functools.partial(residual_kernel, 1.0 / replicas),
        [shape(rank, width), jax.ShapeDtypeStruct((1, units, width), BF16)],
        [right, turned, grads, wide, maps],
        [pltpu.VMEM((32, part), F32), pltpu.VMEM((units, width), BF16), sems((ways,))],
        2 * tokens * units * width,
        dict(in_specs=[vmem] * 5, out_specs=[vmem, hbm]),
    )
    return basis, factor, residual


def solution(mesh):
    replicas, ways = mesh.devices.shape
    far = 8 if replicas % 8 == 0 else 1
    split = Mesh(mesh.devices.reshape(far, replicas // far, ways), ("far", "near", "mp"))
    dp = ("far", "near")
    return jax.shard_map(
        local,
        mesh=split,
        in_specs=(P(dp, "mp"), P(dp, "mp"), P()),
        out_specs=(P(None, "mp"), P(), P(dp, "mp", None)),
        check_vma=False,
    )
```

```python
import functools
import math

import jax
import jax.numpy as jnp
from jax import lax
from jax.experimental import pallas as pl
from jax.experimental.pallas import tpu as pltpu
from jax.sharding import Mesh
from jax.sharding import PartitionSpec as P

F32 = jnp.float32
BF16 = jnp.bfloat16
VMEM_BYTES = 24 * 1024 * 1024
PIECE_PAIRS = ((0, 0), (0, 1), (1, 0), (0, 2), (1, 1), (2, 0))


def pieces(x):
    high = x.astype(BF16).astype(F32)
    rest = x - high
    middle = rest.astype(BF16).astype(F32)
    low = (rest - middle).astype(BF16).astype(F32)
    return high, middle, low


def spread(out_ref, value):
    out_ref[...] = jnp.broadcast_to(value[None], out_ref.shape)


def fold(product, rank):
    return product[:rank] + (product[rank:2 * rank] + product[2 * rank:3 * rank])


def stack_pieces(x, stack):
    rank = x.shape[0]
    stack[...] = jnp.zeros_like(stack)
    for i, piece in enumerate(pieces(x)):
        stack[rank * i:rank * (i + 1), :] = piece
    return stack[...].astype(BF16)


def coeff_kernel(prev_ref, grads_ref, out_ref, stack):
    width = grads_ref.shape[1]
    start = pl.multiple_of(lax.axis_index("mp") * width, width)
    rows = stack_pieces(prev_ref[:, pl.ds(start, width)], stack)
    product = lax.dot_general(
        rows, grads_ref[...], (((1,), (1,)), ((), ())), preferred_element_type=F32
    )
    spread(out_ref, fold(product, prev_ref.shape[0]))


def left_kernel(parts_ref, acts_ref, out_ref, stack):
    rows = stack_pieces(jnp.sum(parts_ref[...], axis=0), stack)
    product = jnp.dot(rows, acts_ref[...], preferred_element_type=F32)
    spread(out_ref, fold(product, parts_ref.shape[1]))


def sum_kernel(parts_ref, out_ref):
    spread(out_ref, jnp.sum(parts_ref[...], axis=0))


def total(x):
    return jnp.sum(jnp.sum(x, axis=1, keepdims=True), axis=0, keepdims=True)


def inverse_root(square):
    inverse = lax.rsqrt(square)
    return inverse * (1.5 - 0.5 * (square * inverse) * inverse)


def triangle(raw):
    rank = raw.shape[0]
    rows = [raw[k:k + 1] for k in range(rank)]
    lane = lax.broadcasted_iota(jnp.int32, (1, 128), 1)
    lines = [jnp.zeros((1, 128), F32) for _ in range(rank)]
    for j in range(rank):
        square = total(rows[j] * rows[j])
        inverse = jnp.where(square > 0.0, inverse_root(square), 0.0)
        unit = rows[j] * inverse
        lines[j] = jnp.where(lane == j, square * inverse, lines[j])
        for k in range(j + 1, rank):
            weight = total(rows[k] * unit)
            rows[k] = rows[k] - weight * unit
            lines[k] = jnp.where(lane == j, weight, lines[k])
    return lines


def back_kernel(scale, parts_ref, acts_ref, raw_ref, out_ref, stack):
    tokens = acts_ref.shape[0]
    raw = jnp.sum(parts_ref[...], axis=0) * scale
    raw_ref[...] = raw
    rows = stack_pieces(raw, stack)
    product = lax.dot_general(
        rows, acts_ref[...], (((1,), (1,)), ((), ())), preferred_element_type=F32
    )
    ways, rank, _ = out_ref.shape
    result = fold(product, rank)
    out_ref[:, :, :tokens] = jnp.broadcast_to(result[None], (ways, rank, tokens))
    for k, line in enumerate(triangle(raw)):
        out_ref[:, k:k + 1, tokens:] = jnp.broadcast_to(line[None], (ways, 1, 128))


def right_kernel(parts_ref, grads_ref, out_ref, stack):
    tokens = grads_ref.shape[0]
    rows = stack_pieces(jnp.sum(parts_ref[:, :, :tokens], axis=0), stack)
    product = jnp.dot(rows, grads_ref[...], preferred_element_type=F32)
    spread(out_ref, fold(product, parts_ref.shape[1]))


def basis_kernel(
    full_units, parts_ref, raw_ref, acts_ref, basis_ref, wide_ref, map_ref, turned_ref, rows
):
    ways, rank, _ = parts_ref.shape
    tokens = acts_ref.shape[0]
    for k in range(ways):
        for r in range(rank):
            rows[r, k:k + 1, :] = parts_ref[k, r:r + 1, tokens:]
    done, mine, maps = [], [], []
    wide_ref[...] = jnp.zeros_like(wide_ref)
    for k in range(rank):
        raw = rows[k]
        vector = raw
        own = raw_ref[k:k + 1]
        line = [jnp.full((1, 1), 1.0 if j == k else 0.0, F32) for j in range(rank)]
        if k:
            weights = [total(u * raw) for u in done]
            vector = raw - functools.reduce(jnp.add, [w * u for w, u in zip(weights, done)])
            own = own - functools.reduce(jnp.add, [w * u for w, u in zip(weights, mine)])
            for w, earlier in zip(weights, maps):
                line = [a - w * b for a, b in zip(line, earlier)]
        inverse = inverse_root(total(vector * vector) + 1e-06)
        done.append(vector * inverse)
        mine.append(own * inverse)
        maps.append([a * inverse for a in line])
        for j in range(rank):
            map_ref[rank * k + j:rank * k + j + 1, :] = jnp.broadcast_to(maps[k][j], (1, 128))
        basis_ref[k:k + 1, :] = mine[k] * math.sqrt(full_units)
        split = pieces(mine[k])
        for i, (a, _) in enumerate(PIECE_PAIRS):
            wide_ref[rank * i + k:rank * i + k + 1, :] = split[a]
    turned_ref[...] = acts_ref[...].T


def residual_kernel(
    scale, parts_ref, turned_ref, grads_ref, wide_ref, map_ref, factor_ref, out_ref,
    held, rounded, sems,
):
    ways, rank, width = parts_ref.shape
    y = jnp.concatenate([parts_ref[i] for i in range(ways)], axis=1) * scale
    held[...] = jnp.zeros_like(held)
    for k in range(rank):
        line = functools.reduce(
            jnp.add,
            [map_ref[rank * k + j:rank * k + j + 1, 0:1] * y[j:j + 1] for j in range(rank)],
        )
        factor_ref[k:k + 1, :] = line
        split = pieces(line)
        for n, (_, b) in enumerate(PIECE_PAIRS):
            held[rank * n + k:rank * n + k + 1, :] = -split[b]
    left = wide_ref[...].astype(BF16)
    right = held[...].astype(BF16)
    copies = []
    for i in range(ways):
        span = slice(i * width, (i + 1) * width)
        whole = jnp.dot(turned_ref[...], grads_ref[i], preferred_element_type=F32)
        less = lax.dot_general(
            left, right[:, span], (((0,), (0,)), ((), ())), preferred_element_type=F32
        )
        rounded[:, span] = (whole + less).astype(rounded.dtype)
        place = pl.ds(i * width, width)
        copies.append(
            pltpu.make_async_copy(rounded.at[:, place], out_ref.at[0, :, place], sems.at[i])
        )
        copies[-1].start()
    for copy in copies:
        copy.wait()


def call(kernel, outs, args, scratch, flops, grid=None):
    moved = sum(a.size * a.dtype.itemsize for a in args)
    moved += sum(o.size * o.dtype.itemsize for o in outs)
    single = len(outs) == 1
    return pl.pallas_call(
        kernel,
        out_shape=outs[0] if single else outs,
        scratch_shapes=scratch,
        compiler_params=pltpu.CompilerParams(vmem_limit_bytes=VMEM_BYTES),
        cost_estimate=pl.CostEstimate(flops=flops, bytes_accessed=moved, transcendentals=0),
        **(grid or {}),
    )(*args)


def exchange(copies, axis):
    return lax.all_to_all(copies, axis, 0, 0, tiled=True)


def local(hidden_acts, out_grads, prev_factor):
    tokens, units = hidden_acts.shape
    rank, width = prev_factor.shape
    ways, near, far = (lax.axis_size(a) for a in ("mp", "near", "far"))
    replicas = near * far
    part = width // ways
    rows = lambda n: pltpu.VMEM((16, n), F32)
    shape = lambda *dims: jax.ShapeDtypeStruct(dims, F32)

    grads = lax.all_gather(out_grads, "mp", axis=0)
    hbm = pl.BlockSpec(memory_space=pltpu.HBM)
    vmem = pl.BlockSpec(memory_space=pltpu.VMEM)
    sems = pltpu.SemaphoreType.DMA

    coeffs = call(
        coeff_kernel, [shape(ways, rank, tokens)], [prev_factor, out_grads],
        [rows(part)], 32 * tokens * part,
    )
    left = call(
        left_kernel, [shape(near, rank, units)], [exchange(coeffs, "mp"), hidden_acts],
        [rows(tokens)], 32 * tokens * units,
    )
    left = call(sum_kernel, [shape(far, rank, units)], [exchange(left, "near")], [], 8 * units)
    raw, packed = call(
        functools.partial(back_kernel, 1.0 / replicas),
        [shape(rank, units), shape(ways, rank, tokens + 128)],
        [exchange(left, "far"), hidden_acts], [rows(units)], 32 * tokens * units,
    )
    packed = exchange(packed, "mp")
    right = call(
        right_kernel, [shape(near, rank, part)], [packed, out_grads],
        [rows(tokens)], 32 * tokens * part,
    )
    basis, wide, maps, turned = call(
        functools.partial(basis_kernel, units * ways),
        [
            shape(rank, units), shape(32, units), shape(rank * rank, 128),
            jax.ShapeDtypeStruct((units, tokens), BF16),
        ],
        [packed, raw, hidden_acts], [pltpu.VMEM((rank, ways, 128), F32)], 100 * ways * units,
    )
    right = call(sum_kernel, [shape(far, rank, part)], [exchange(right, "near")], [], 8 * part)
    right, grads = lax.optimization_barrier((exchange(right, "far"), grads))
    right = call(sum_kernel, [shape(ways, rank, part)], [right], [], 8 * part)
    right = exchange(right, "mp")

    factor, residual = call(
        functools.partial(residual_kernel, 1.0 / replicas),
        [shape(rank, width), jax.ShapeDtypeStruct((1, units, width), BF16)],
        [right, turned, grads, wide, maps],
        [pltpu.VMEM((32, width), F32), pltpu.VMEM((units, width), BF16), sems((ways,))],
        2 * tokens * units * width,
        dict(in_specs=[vmem] * 5, out_specs=[vmem, hbm]),
    )
    return basis, factor, residual


def solution(mesh):
    replicas, ways = mesh.devices.shape
    far = 8 if replicas % 8 == 0 else 1
    split = Mesh(mesh.devices.reshape(far, replicas // far, ways), ("far", "near", "mp"))
    dp = ("far", "near")
    return jax.shard_map(
        local,
        mesh=split,
        in_specs=(P(dp, "mp"), P(dp, "mp"), P()),
        out_specs=(P(None, "mp"), P(), P(dp, "mp", None)),
        check_vma=False,
    )
```
